1024 devices in a mesh: elem: 128 (over y, z, core), band: 8 (over x).
Axes of the slice: x: 8, y: 8, z: 8, core: 2. Of those that a mesh axis runs over, the one named last changes fastest.
Arguments:
- psi: bfloat16 [2, 128, 4096, 240], P(None, 'elem', 'band'), may hold values from -6 to 6
- h_diag: bfloat16 [128, 240, 240], P('elem'), may hold values from -0.375 to 0.375
- h_face: bfloat16 [128, 6, 240, 240], P('elem'), may hold values from -0.375 to 0.375
- adjacency: int32 [128, 6], P('elem'), may hold values from 0 to 127, as said below
- nbasis: int32 [128], P('elem'), may hold values from 60 to 240
Outputs:
- psi_next: bfloat16 [2, 128, 4096, 240], P(None, 'elem', 'band')
- intersection: float32 [512, 2, 4096], P('elem', None, 'band')
- density: float32 [128, 240], P('elem')
The draws below stay inside these ranges and needn't reach their ends.
Inputs may be any that keep to these rules, and one draw needn't show every extreme that they name: `adjacency`: the neighbour across each face lies in the same block of 1 consecutive elements as the element, in the previous block or in the next one, counted cyclically; face 0 always in the previous block, face 1 always in the next.
All inputs are finite; a program needn't handle non-finite values.
Results may differ from the reference program's by a relative error of at most 0.0032.
Values may be sent and summed in bfloat16 or wider, within the bound.
A program may use at most 32 MiB of HBM per device.

```python
import jax
import jax.numpy as jnp
from jax import lax

BASIS = 240
ORBS = 4096
FACES = 6
E_DEV = 1
ITERS = 2
ELEMS = 128
GROUP = 512
N_BAND = 8


def draw_adjacency(key, part):
    first_key, second_key = jax.random.split(jax.random.fold_in(key, 11))
    blocks = ELEMS // E_DEV
    home = jnp.arange(ELEMS, dtype=jnp.int32) // E_DEV
    face_number = jnp.arange(FACES, dtype=jnp.int32)[None, :]
    offset = jax.random.randint(first_key, (ELEMS, FACES), -1, 2, dtype=jnp.int32)
    offset = jnp.where(face_number == 0, -1, jnp.where(face_number == 1, 1, offset))
    within = jax.random.randint(second_key, (ELEMS, FACES), 0, E_DEV, dtype=jnp.int32)
    return (jnp.mod(home[:, None] + offset, blocks) * E_DEV + within).astype(jnp.int32)


def draw_nbasis(key, part):
    sizes_drawn = jax.random.randint(jax.random.fold_in(key, 23), (ELEMS,), BASIS // 4, BASIS + 1, dtype=jnp.int32)
    sizes_drawn = sizes_drawn.at[0].set(BASIS).at[1].set(BASIS // 4)
    return sizes_drawn


def block_levels(own_key, dims, cuts, low, top_value):
    level, own = 1.0, jax.random.fold_in(own_key, 6)
    for dim, shards_of in cuts:
        draws = jnp.exp(jax.random.uniform(jax.random.fold_in(own, dim), (shards_of,), jnp.float32, low / len(cuts), top_value / len(cuts)))
        level = level * jnp.repeat(draws, dims[dim] // shards_of).reshape([-1 if axis == dim else 1 for axis in range(len(dims))])
    return level


def gaussian(own_key, shape, spread, reach, pieces=(), kind=jnp.bfloat16):
    result = spread * jax.random.normal(own_key, shape, jnp.float32)
    if pieces:
        result = result * block_levels(own_key, shape, pieces, -0.22, 0.18)
    return jnp.clip(result, -reach, reach).astype(kind)


def setup_inputs(seed: int = 0) -> dict:
    splits = jax.random.split(jax.random.key(seed), 6)
    return {
        "psi": gaussian(splits[0], (2, ELEMS, ORBS, BASIS), 1.0, 6.0, ((1, 128), (2, 8))),
        "h_diag": gaussian(splits[1], (ELEMS, BASIS, BASIS), BASIS ** -0.5, 0.375, ((0, 128),)),
        "h_face": gaussian(splits[2], (ELEMS, FACES, BASIS, BASIS), BASIS ** -0.5, 0.375, ((0, 128),)),
        "adjacency": draw_adjacency(jax.random.fold_in(splits[5], 71), 0),
        "nbasis": draw_nbasis(jax.random.fold_in(splits[5], 71), 0),
    }


half_step = 0.1


def reference(psi, h_diag, h_face, adjacency, nbasis):
    mask = jnp.arange(BASIS, dtype=jnp.int32)[None, :] < nbasis[:, None]
    psi0 = jnp.where(mask[None, :, None, :], psi, jnp.zeros_like(psi))
    state = psi0
    for sweep_index in range(ITERS):
        total = (psi0.astype(jnp.float32) + state.astype(jnp.float32)).astype(jnp.bfloat16)

        def one_element(element):
            own = total[:, element].reshape(2 * ORBS, BASIS)
            image = jnp.dot(own, h_diag[element].T, preferred_element_type=jnp.float32).reshape(2, ORBS, BASIS)
            near = jnp.take(total, adjacency[element], axis=1)
            image = image + jnp.einsum('cfob,fkb->cok', near.astype(jnp.float32), h_face[element].astype(jnp.float32))
            keep = mask[element][None, None, :]
            image = jnp.where(keep, image, jnp.zeros_like(image))
            base = psi0[:, element].astype(jnp.float32)
            real_part = base[0] + half_step * image[1]
            imag_part = base[1] - half_step * image[0]
            return jnp.stack([real_part, imag_part]).astype(jnp.bfloat16)

        state = jnp.moveaxis(lax.map(one_element, jnp.arange(ELEMS, dtype=jnp.int32)), 0, 1)
    squares_sum = jnp.sum(jnp.square(state.astype(jnp.float32)), axis=(0, 2))
    density = squares_sum * (1.0 / ORBS)
    grouped = state.reshape(2, ELEMS, N_BAND, GROUP, BASIS)
    grouped = jnp.transpose(grouped, (2, 0, 3, 1, 4)).reshape(N_BAND, 2, GROUP, ELEMS * BASIS)

    def one_group(block):
        real_rows = block[0]
        imag_rows = block[1]
        sum_real = jnp.dot(real_rows, real_rows.T, preferred_element_type=jnp.float32) + jnp.dot(imag_rows, imag_rows.T, preferred_element_type=jnp.float32)
        sum_imag = jnp.dot(imag_rows, real_rows.T, preferred_element_type=jnp.float32) - jnp.dot(real_rows, imag_rows.T, preferred_element_type=jnp.float32)
        return jnp.stack([sum_real, sum_imag], axis=1)

    blocks = lax.map(one_group, grouped)
    intersection = jnp.transpose(blocks, (1, 2, 0, 3)).reshape(GROUP, 2, ORBS) * (1.0 / (ELEMS * BASIS))
    return state, intersection, density
```

```python
import functools

import jax
import jax.numpy as jnp
from jax import lax
from jax.experimental import pallas as pl
from jax.experimental.pallas import tpu as pltpu
from jax.sharding import PartitionSpec as P

MESH = pl.DeviceIdType.MESH
F32 = jnp.float32
BF16 = jnp.bfloat16
HALF_STEP = 0.1


def dot(a, b):
    return jnp.dot(a, b, preferred_element_type=F32)


def dot_nt(a, b):
    return lax.dot_general(a, b, (((1,), (1,)), ((), ())), preferred_element_type=F32)


def kernel(
    side, bands, chunks, adj, nb, psi, hd, hf, out_psi, out_int, out_den,
    psi_v, hd_v, hf_v, hm, t0, t0f, t0n, t1, t1f, t1n, xo, xp, pick, sel, own, gs, gr, s2, s2r, dac, dens, denr,
    load_sem, out_sem, h_send, h_recv, p_send, p_recv, g_send, g_recv, r_send, r_recv, d_send, d_recv,
):
    elems = side * side * 2
    faces = hf.shape[0]
    basis = hd.shape[0]
    group = xo.shape[2]
    width = group // chunks
    peers = side - 1
    turn = [side // 2 + (k // 2 if k % 2 == 0 else -(k + 1) // 2) for k in range(side)]

    e = lax.axis_index("elem")
    band = lax.axis_index("band")
    core = e % 2
    chip = e // 2
    y, z = chip // side, chip % side
    far = (e + elems - 1 + 2 * core) % elems
    near = e + 1 - 2 * core

    def along(first, r):
        by_y = core if not first else 1 - core
        yy = (y + by_y * r) % side
        zz = (z + (1 - by_y) * r) % side
        return (yy * side + zz) * 2 + core

    firsts = [along(True, r) for r in turn[:-1]]
    seconds = [along(False, r) for r in turn[:-1]]
    others = [(band + r) % bands for r in range(1, bands)]

    loads = []
    for i in range(chunks):
        for c in range(2):
            copy = pltpu.make_async_copy(
                psi.at[c, :, pl.ds(i * width, width)], psi_v.at[i, :, pl.ds(c * width, width)], load_sem.at[2 * i + c]
            )
            copy.start()
            loads.append(copy)
    load_hd = pltpu.make_async_copy(hd, hd_v, load_sem.at[2 * chunks])
    load_hf = pltpu.make_async_copy(hf, hf_v, load_sem.at[2 * chunks + 1])
    load_hd.start()
    load_hf.start()

    barrier = pltpu.get_barrier_semaphore()
    everyone = [(far, band), (near, band)]
    everyone += [(d, band) for d in firsts + seconds]
    everyone += [(e, b) for b in others]
    for d in everyone:
        pl.semaphore_signal(barrier, inc=1, device_id=d, device_id_type=MESH)

    block = group // 2 // side
    t = lax.broadcasted_iota(jnp.int32, (group // 2, group), 0)
    o = lax.broadcasted_iota(jnp.int32, (group // 2, group), 1)
    k = t // block
    r = side // 2 + jnp.where(k % 2 == 0, k // 2, 0 - (k + 1) // 2)
    position = (1 - core) * y + core * z
    d = (position + r) % side
    j = t % block
    q = j // 4
    orbital = ((1 - core) * (d * side + q) + core * (q * side + d)) * 8 + core * 4 + j % 4
    pick[...] = jnp.where(orbital == o, 1.0, 0.0).astype(BF16)

    keep = lax.broadcasted_iota(jnp.int32, (basis, 2 * width), 0) < nb[0]

    pl.semaphore_wait(barrier, len(everyone))

    def halo(sweep, i, src, dst, to_far):
        s = (sweep * 2 + to_far) * chunks + i
        return pltpu.make_async_remote_copy(
            src_ref=src.at[i], dst_ref=dst.at[i], send_sem=h_send.at[s], recv_sem=h_recv.at[s],
            device_id=(far if to_far else near, band), device_id_type=MESH,
        )

    sent = []
    for i in range(chunks):
        loads[2 * i].wait()
        loads[2 * i + 1].wait()
        t0[i] = jnp.where(keep, psi_v[i].astype(F32), 0.0).astype(BF16)
        for copy in (halo(0, i, t0, t0f, 1), halo(0, i, t0, t0n, 0)):
            copy.start()
            sent.append(copy)

    load_hd.wait()
    load_hf.wait()
    weights = [[jnp.where(adj[0, f] == s, 1.0, 0.0).astype(F32) for f in range(faces)] for s in (e, far, near)]
    strip = 16

    def prepare(n, carry):
        rows = pl.ds(pl.multiple_of(n * strip, strip), strip)
        low = pl.ds(pl.multiple_of(basis + n * strip, strip), strip)
        valid = lax.broadcasted_iota(jnp.int32, (strip, basis), 0) + n * strip < nb[0]
        faces_f32 = [hf_v[f, rows, :].astype(F32) for f in range(faces)]
        for s in range(3):
            total = hd_v[rows, :].astype(F32) if s == 0 else jnp.zeros((strip, basis), F32)
            for f in range(faces):
                total = total + weights[s][f] * faces_f32[f]
            total = jnp.where(valid, total, 0.0)
            high = total.astype(BF16)
            hm[s, rows, :] = high
            hm[s, low, :] = (total - high.astype(F32)).astype(BF16)
        return carry

    lax.fori_loop(0, basis // strip, prepare, 0)

    def image(i, mine, other, beside):
        both = dot(hm[0], mine[i]) + dot(hm[1], other[i]) + dot(hm[2], beside[i])
        return both[:basis] + both[basis:]

    for i in range(chunks):
        halo(0, i, t0, t0n, 0).wait_recv()
        halo(0, i, t0, t0f, 1).wait_recv()
        im = image(i, t0, t0f, t0n)
        base = t0[i].astype(F32)
        turned = jnp.concatenate([im[:, width:], -im[:, :width]], axis=1)
        state = (base + (2 * HALF_STEP) * turned).astype(BF16)
        t1[i] = (base + state.astype(F32)).astype(BF16)
        for copy in (halo(1, i, t1, t1f, 1), halo(1, i, t1, t1n, 0)):
            copy.start()
            sent.append(copy)

    def to_partner(i):
        lanes = pl.ds(i * width, width)
        return pltpu.make_async_remote_copy(
            src_ref=xo.at[:, :, lanes], dst_ref=xp.at[:, :, lanes], send_sem=p_send.at[i], recv_sem=p_recv.at[i],
            device_id=(near, band), device_id_type=MESH,
        )

    stores = []
    dac[...] = jnp.zeros_like(dac)
    for i in range(chunks):
        halo(1, i, t1, t1n, 0).wait_recv()
        halo(1, i, t1, t1f, 1).wait_recv()
        im = image(i, t1, t1f, t1n)
        base = t0[i].astype(F32)
        lanes = pl.ds(i * width, width)
        real = (base[:, :width] + HALF_STEP * im[:, width:]).astype(BF16)
        imag = (base[:, width:] - HALF_STEP * im[:, :width]).astype(BF16)
        xo[0, :, lanes] = real
        xo[1, :, lanes] = imag
        copy = to_partner(i)
        copy.start()
        sent.append(copy)
        copy = pltpu.make_async_copy(xo.at[:, :, lanes], out_psi.at[:, :, lanes], out_sem.at[i])
        copy.start()
        stores.append(copy)
        real, imag = real.astype(F32), imag.astype(F32)
        dac[:basis, :] += real * real + imag * imag

    column = jnp.transpose(dac[...])
    part = column[0:8]
    for n in range(1, width // 8):
        part = part + column[8 * n : 8 * n + 8]
    dens[...] = part
    for n in range(bands - 1):
        copy = pltpu.make_async_remote_copy(
            src_ref=dens, dst_ref=denr.at[n], send_sem=d_send.at[n], recv_sem=d_recv.at[n],
            device_id=(e, others[n]), device_id_type=MESH,
        )
        copy.start()
        sent.append(copy)

    for c in range(2):
        sel[c] = dot_nt(pick[...], xo[c]).astype(BF16)
    for i in range(chunks):
        to_partner(i).wait_recv()
    for c in range(2):
        sel[2 + c] = dot_nt(pick[...], xp[c]).astype(BF16)

    def first(k):
        return pltpu.make_async_remote_copy(
            src_ref=gs.at[k], dst_ref=gr.at[k], send_sem=g_send.at[k], recv_sem=g_recv.at[k],
            device_id=(firsts[k], band), device_id_type=MESH,
        )

    per = max(side // 2, 1)
    for h in range(side // per):
        rows = pl.ds(h * per * block, per * block)
        total = None
        for source, at in ((xo, 0), (xp, 2)):
            left, right = sel[at, rows, :], sel[at + 1, rows, :]
            term = dot(jnp.concatenate([left, right], axis=0), source[0])
            term = term + dot(jnp.concatenate([right, -left], axis=0), source[1])
            total = term if total is None else total + term
        for b in range(per):
            k = h * per + b
            a = slice(b * block, (b + 1) * block)
            c = slice((per + b) * block, (per + b + 1) * block)
            if k < peers:
                gs[k, :block, :] = total[a].astype(BF16)
                gs[k, block:, :] = total[c].astype(BF16)
                copy = first(k)
                copy.start()
                sent.append(copy)
            else:
                own[:block, :] = total[a]
                own[block:, :] = total[c]

    for k in range(peers):
        first(k).wait_recv()
    upper = lax.broadcasted_iota(jnp.int32, (8, group), 0) < 4
    for m in range(block // 8):
        tiles = []
        for at in (8 * m, block + 8 * m):
            tile = own[at : at + 8, :]
            for k in range(peers):
                tile = tile + gr[k, at : at + 8, :].astype(F32)
            tiles.append(tile)
        s2[2 * m] = jnp.where(upper, tiles[0], pltpu.roll(tiles[1], 4, 0))
        s2[2 * m + 1] = jnp.where(upper, pltpu.roll(tiles[0], 4, 0), tiles[1])

    place = core * y + (1 - core) * z

    def second(k):
        return pltpu.make_async_remote_copy(
            src_ref=s2.at[(place + turn[k]) % side], dst_ref=s2r.at[k], send_sem=r_send.at[k], recv_sem=r_recv.at[k],
            device_id=(seconds[k], band), device_id_type=MESH,
        )

    for k in range(peers):
        copy = second(k)
        copy.start()
        sent.append(copy)
    part = dens[...]
    for n in range(bands - 1):
        pltpu.make_async_remote_copy(
            src_ref=dens, dst_ref=denr.at[n], send_sem=d_send.at[n], recv_sem=d_recv.at[n],
            device_id=(e, others[n]), device_id_type=MESH,
        ).wait_recv()
        part = part + denr[n]
    whole = jnp.sum(part, axis=0, keepdims=True) * (1.0 / (group * bands))
    out_den[...] = whole[:, :basis]
    result = s2[place]
    for k in range(peers):
        second(k).wait_recv()
        result = result + s2r[k]
    result = result * (1.0 / (elems * basis))
    for n in range(4):
        out_int[n, 0:1, :] = result[n : n + 1]
        out_int[n, 1:2, :] = result[4 + n : 5 + n]

    for copy in stores:
        copy.wait()
    for copy in sent:
        copy.wait_send()


def shards(side, bands, chunks, psi, h_diag, h_face, adjacency, nbasis):
    group, basis = psi.shape[2], psi.shape[3]
    faces = h_face.shape[1]
    width = group // chunks
    half = group // 2
    block = half // side
    peers = side - 1
    dma = pltpu.SemaphoreType.DMA
    anywhere = pl.BlockSpec(memory_space=pl.ANY)
    hbm = pl.BlockSpec(memory_space=pltpu.HBM)
    scalars = pl.BlockSpec(memory_space=pltpu.SMEM)
    vmem = pl.BlockSpec(memory_space=pltpu.VMEM)
    chunked = pltpu.VMEM((chunks, basis, 2 * width), BF16)
    out_psi, out_int, out_den = pl.pallas_call(
        functools.partial(kernel, side, bands, chunks),
        out_shape=(
            jax.ShapeDtypeStruct((2, basis, group), BF16),
            jax.ShapeDtypeStruct((4, 2, group), F32),
            jax.ShapeDtypeStruct((1, basis), F32),
        ),
        in_specs=[scalars, scalars, hbm, hbm, hbm],
        out_specs=(anywhere, vmem, vmem),
        scratch_shapes=[
            chunked,
            pltpu.VMEM((basis, basis), BF16),
            pltpu.VMEM((faces, basis, basis), BF16),
            pltpu.VMEM((3, 2 * basis, basis), BF16),
            *[chunked] * 6,
            pltpu.VMEM((2, basis, group), BF16),
            pltpu.VMEM((2, basis, group), BF16),
            pltpu.VMEM((half, group), BF16),
            pltpu.VMEM((4, half, basis), BF16),
            pltpu.VMEM((2 * block, group), F32),
            pltpu.VMEM((peers, 2 * block, group), BF16),
            pltpu.VMEM((peers, 2 * block, group), BF16),
            pltpu.VMEM((side, 8, group), F32),
            pltpu.VMEM((peers, 8, group), F32),
            pltpu.VMEM((256, width), F32),
            pltpu.VMEM((8, 256), F32),
            pltpu.VMEM((bands - 1, 8, 256), F32),
            dma((2 * chunks + 2,)),
            dma((chunks,)),
            dma((4 * chunks,)),
            dma((4 * chunks,)),
            dma((chunks,)),
            dma((chunks,)),
            dma((peers,)),
            dma((peers,)),
            dma((peers,)),
            dma((peers,)),
            dma((bands - 1,)),
            dma((bands - 1,)),
        ],
        compiler_params=pltpu.CompilerParams(
            collective_id=0, has_side_effects=True, vmem_limit_bytes=62 * 10**6
        ),
        name="step",
    )(
        adjacency,
        nbasis,
        jnp.transpose(psi, (1, 0, 3, 2))[0],
        h_diag[0],
        h_face[0],
    )
    return jnp.transpose(out_psi, (0, 2, 1))[:, None], out_int, out_den


def build(mesh, side, chunks):
    bands = mesh.shape["band"]
    return jax.shard_map(
        functools.partial(shards, side, bands, chunks),
        mesh=mesh,
        in_specs=(
            P(None, "elem", "band", None),
            P("elem", None, None),
            P("elem", None, None, None),
            P("elem", None),
            P("elem"),
        ),
        out_specs=(P(None, "elem", "band", None), P("elem", None, "band"), P("elem", None)),
        check_vma=False,
    )


def solution(mesh):
    return build(mesh, 8, 4)
```

```python
import functools

import jax
import jax.numpy as jnp
from jax import lax
from jax.experimental import pallas as pl
from jax.experimental.pallas import tpu as pltpu
from jax.sharding import PartitionSpec as P

MESH = pl.DeviceIdType.MESH
F32 = jnp.float32
BF16 = jnp.bfloat16
HALF_STEP = 0.1


def dot(a, b):
    return jnp.dot(a, b, preferred_element_type=F32)


def dot_nt(a, b):
    return lax.dot_general(a, b, (((1,), (1,)), ((), ())), preferred_element_type=F32)


def kernel(
    side, bands, chunks, pieces, adj_h, nb_h, psi, hd, hf, out_psi, out_int, out_den,
    adj, nb, psi_v, hd_v, hf_v, hm, t0, t0f, t0n, t1, t1f, t1n, xo, xp, pick, sel, own, gs, gr, s2, s2r, dac, dens,
    load_sem, few_sem, out_sem, h_send, h_recv, p_send, p_recv, g_send, g_recv, r_send, r_recv, d_send, d_recv,
):
    elems = side * side * 2
    faces = hf.shape[0]
    basis = hd.shape[0]
    group = xo.shape[2]
    width = group // chunks
    peers = side - 1
    turn = [side // 2 + (k // 2 if k % 2 == 0 else -(k + 1) // 2) for k in range(side)]

    e = lax.axis_index("elem")
    band = lax.axis_index("band")
    core = e % 2
    chip = e // 2
    y, z = chip // side, chip % side
    far = (e + elems - 1 + 2 * core) % elems
    near = e + 1 - 2 * core

    def along(first, r):
        by_y = core if not first else 1 - core
        yy = (y + by_y * r) % side
        zz = (z + (1 - by_y) * r) % side
        return (yy * side + zz) * 2 + core

    firsts = [along(True, r) for r in turn[:-1]]
    seconds = [along(False, r) for r in range(1, side)]
    reach = [r for r in (1, 2, -1, -2) if abs(r) < bands]
    if bands <= 3:
        reach = [1, -1][: bands - 1]

    barrier = pltpu.get_barrier_semaphore()
    everyone = [(far, band), (near, band)]
    everyone += [(d, band) for d in firsts + seconds]
    everyone += [(e, (band + r) % bands) for r in reach]
    for d in everyone:
        pl.semaphore_signal(barrier, inc=1, device_id=d, device_id_type=MESH)

    load_adj = pltpu.make_async_copy(adj_h, adj, few_sem.at[1])
    load_adj.start()
    loads = []
    for i in range(chunks):
        for c in range(2):
            copy = pltpu.make_async_copy(
                psi.at[c, :, pl.ds(i * width, width)], psi_v.at[i, :, pl.ds(c * width, width)], load_sem.at[2 * i + c]
            )
            copy.start()
            loads.append(copy)
    load_hd = pltpu.make_async_copy(hd, hd_v, load_sem.at[2 * chunks])
    load_hf = pltpu.make_async_copy(hf, hf_v, load_sem.at[2 * chunks + 1])
    load_hd.start()
    load_hf.start()

    keep = lax.broadcasted_iota(jnp.int32, (basis, 2 * width), 0) < nb_h[0]

    def halo(sweep, i, src, dst, to_far):
        s = (sweep * 2 + to_far) * chunks + i
        return pltpu.make_async_remote_copy(
            src_ref=src.at[i], dst_ref=dst.at[i], send_sem=h_send.at[s], recv_sem=h_recv.at[s],
            device_id=(far if to_far else near, band), device_id_type=MESH,
        )

    sent = []
    for i in range(chunks):
        loads[2 * i].wait()
        loads[2 * i + 1].wait()
        t0[i] = jnp.where(keep, psi_v[i].astype(F32), 0.0).astype(BF16)
        if i == 0:
            pl.semaphore_wait(barrier, len(everyone))
        for copy in (halo(0, i, t0, t0f, 1), halo(0, i, t0, t0n, 0)):
            copy.start()
            sent.append(copy)

    load_hd.wait()
    load_hf.wait()
    load_adj.wait()
    weights = [[jnp.where(adj[0, f] == s, 1.0, 0.0).astype(F32) for f in range(faces)] for s in (e, far, near)]
    strip = 16

    def prepare(n, carry):
        rows = pl.ds(pl.multiple_of(n * strip, strip), strip)
        low = pl.ds(pl.multiple_of(basis + n * strip, strip), strip)
        valid = lax.broadcasted_iota(jnp.int32, (strip, basis), 0) + n * strip < nb_h[0]
        faces_f32 = [hf_v[f, rows, :].astype(F32) for f in range(faces)]
        for s in range(3):
            total = hd_v[rows, :].astype(F32) if s == 0 else jnp.zeros((strip, basis), F32)
            for f in range(faces):
                total = total + weights[s][f] * faces_f32[f]
            total = jnp.where(valid, total, 0.0)
            high = total.astype(BF16)
            hm[s, rows, :] = high
            hm[s, low, :] = (total - high.astype(F32)).astype(BF16)
        return carry

    lax.fori_loop(0, basis // strip, prepare, 0)

    def image(sweep, i, mine, other, beside):
        halo(sweep, i, mine, beside, 0).wait_recv()
        both = dot(hm[0], mine[i]) + dot(hm[2], beside[i])
        halo(sweep, i, mine, other, 1).wait_recv()
        both = both + dot(hm[1], other[i])
        return both[:basis] + both[basis:]

    for i in range(chunks):
        im = image(0, i, t0, t0f, t0n)
        base = t0[i].astype(F32)
        turned = jnp.concatenate([im[:, width:], -im[:, :width]], axis=1)
        state = (base + (2 * HALF_STEP) * turned).astype(BF16)
        t1[i] = (base + state.astype(F32)).astype(BF16)
        for copy in (halo(1, i, t1, t1f, 1), halo(1, i, t1, t1n, 0)):
            copy.start()
            sent.append(copy)

    block = group // 2 // side
    part = block // pieces
    slab = min(group, 128)
    t = lax.broadcasted_iota(jnp.int32, (group // 2, slab), 0)
    o = lax.broadcasted_iota(jnp.int32, (group // 2, slab), 1)

    def split(v, size):
        return v >> (size.bit_length() - 1), v & (size - 1)

    k, j = split(t, part)
    h, k = split(k, side)
    up, odd = split(k, 2)
    r = side // 2 + jnp.where(odd == 0, up, -1 - up)
    d = ((1 - core) * y + core * z + r) & (side - 1)
    q, four = split(h * part + j, 4)
    orbital = ((1 - core) * (d * side + q) + core * (q * side + d)) * 8 + core * 4 + four
    for n in range(group // slab):
        pick[:, n * slab : (n + 1) * slab] = jnp.where(orbital == o + n * slab, 1.0, 0.0).astype(BF16)

    def to_partner(i):
        lanes = pl.ds(i * width, width)
        return pltpu.make_async_remote_copy(
            src_ref=xo.at[:, :, lanes], dst_ref=xp.at[:, :, lanes], send_sem=p_send.at[i], recv_sem=p_recv.at[i],
            device_id=(near, band), device_id_type=MESH,
        )

    stores = []
    dac[...] = jnp.zeros_like(dac)
    for i in range(chunks):
        im = image(1, i, t1, t1f, t1n)
        base = t0[i].astype(F32)
        lanes = pl.ds(i * width, width)
        real = (base[:, :width] + HALF_STEP * im[:, width:]).astype(BF16)
        imag = (base[:, width:] - HALF_STEP * im[:, :width]).astype(BF16)
        xo[0, :, lanes] = real
        xo[1, :, lanes] = imag
        copy = to_partner(i)
        copy.start()
        sent.append(copy)
        copy = pltpu.make_async_copy(xo.at[:, :, lanes], out_psi.at[:, :, lanes], out_sem.at[i])
        copy.start()
        stores.append(copy)
        real, imag = real.astype(F32), imag.astype(F32)
        dac[:basis, :] += real * real + imag * imag

    column = jnp.transpose(dac[...])
    some = column[0:8]
    for n in range(1, width // 8):
        some = some + column[8 * n : 8 * n + 8]
    dens[band] = some

    def density(n, to, slot):
        slot = (band + slot) % bands
        return pltpu.make_async_remote_copy(
            src_ref=dens.at[slot], dst_ref=dens.at[slot], send_sem=d_send.at[n], recv_sem=d_recv.at[n],
            device_id=(e, (band + to) % bands), device_id_type=MESH,
        )

    for n, r in enumerate(reach):
        copy = density(n, r, 0)
        copy.start()
        sent.append(copy)
    passed = [(2, -2), (2, -1), (-2, 1)] if bands == 8 else []

    for c in range(2):
        sel[c] = dot_nt(pick[...], xo[c]).astype(BF16)
    for i in range(chunks):
        to_partner(i).wait_recv()
    for c in range(2):
        sel[2 + c] = dot_nt(pick[...], xp[c]).astype(BF16)

    def first(h, k):
        s = h * peers + k
        return pltpu.make_async_remote_copy(
            src_ref=gs.at[s], dst_ref=gr.at[s], send_sem=g_send.at[s], recv_sem=g_recv.at[s],
            device_id=(firsts[k], band), device_id_type=MESH,
        )

    high = side * part
    for h in range(pieces):
        rows = pl.ds(h * high, high)
        total = None
        for source, at in ((xo, 0), (xp, 2)):
            left, right = sel[at, rows, :], sel[at + 1, rows, :]
            term = dot(jnp.concatenate([left, right], axis=0), source[0])
            term = term + dot(jnp.concatenate([right, -left], axis=0), source[1])
            total = term if total is None else total + term
        for k in range(side):
            both = jnp.concatenate(
                [total[k * part : (k + 1) * part], total[high + k * part : high + (k + 1) * part]], axis=0
            )
            if k < peers:
                gs[h * peers + k] = both.astype(BF16)
                copy = first(h, k)
                copy.start()
                sent.append(copy)
            else:
                own[h] = both

    place = core * y + (1 - core) * z
    upper = lax.broadcasted_iota(jnp.int32, (8, group), 0) < 4

    def second(q, r):
        return pltpu.make_async_remote_copy(
            src_ref=s2.at[q], dst_ref=s2r.at[r - 1], send_sem=r_send.at[r - 1], recv_sem=r_recv.at[r - 1],
            device_id=(along(False, r), band), device_id_type=MESH,
        )

    for h in range(pieces):
        for k in range(peers):
            first(h, k).wait_recv()
        for m in range(part // 8):
            tiles = []
            for at in (8 * m, part + 8 * m):
                tile = own[h, at : at + 8, :]
                for k in range(peers):
                    tile = tile + gr[h * peers + k, at : at + 8, :].astype(F32)
                tiles.append(tile)
            q = h * (part // 4) + 2 * m
            for to, tile in (
                (q, jnp.where(upper, tiles[0], pltpu.roll(tiles[1], 4, 0))),
                (q + 1, jnp.where(upper, pltpu.roll(tiles[0], 4, 0), tiles[1])),
            ):
                s2[to] = jnp.concatenate([tile[:, : group // 2], tile[:, group // 2 :]], axis=0).astype(BF16)
            for to in (q, q + 1):
                r = (to + side - place) % side

                @pl.when(r != 0)
                def _(to=to, r=r):
                    second(to, r).start()

        if h == 0:
            for n, r in enumerate(reach):
                density(n, r, -r).wait_recv()
            for n, (to, slot) in enumerate(passed):
                copy = density(len(reach) + n, to, slot)
                copy.start()
                sent.append(copy)

    result = s2[place].astype(F32)
    for r in range(1, side):
        second((place + r) % side, r).wait_recv()
        result = result + s2r[r - 1].astype(F32)
    result = jnp.concatenate([result[:8], result[8:]], axis=1) * (1.0 / (elems * basis))
    for n in range(4):
        out_int[n, 0:1, :] = result[n : n + 1]
        out_int[n, 1:2, :] = result[4 + n : 5 + n]
    for n, (to, slot) in enumerate(passed):
        density(len(reach) + n, to, slot - to).wait_recv()
    some = dens[0]
    for n in range(1, bands):
        some = some + dens[n]
    whole = jnp.sum(some, axis=0, keepdims=True) * (1.0 / (group * bands))
    out_den[...] = whole[:, :basis]

    for r in range(1, side):
        second((place + r) % side, r).wait_send()
    for copy in stores:
        copy.wait()
    for copy in sent:
        copy.wait_send()


def finish(*refs):
    copies = [pltpu.make_async_copy(refs[n], refs[3 + n], refs[6].at[n]) for n in range(3)]
    for copy in copies:
        copy.start()
    for copy in copies:
        copy.wait()


def shards(side, bands, chunks, pieces, psi, h_diag, h_face, adjacency, nbasis):
    group, basis = psi.shape[2], psi.shape[3]
    faces = h_face.shape[1]
    width = group // chunks
    half = group // 2
    block = half // side
    peers = side - 1
    dma = pltpu.SemaphoreType.DMA
    anywhere = pl.BlockSpec(memory_space=pl.ANY)
    hbm = pl.BlockSpec(memory_space=pltpu.HBM)
    vmem = pl.BlockSpec(memory_space=pltpu.VMEM)
    chunked = pltpu.VMEM((chunks, basis, 2 * width), BF16)
    arguments = [adjacency, nbasis, jnp.transpose(psi, (1, 0, 3, 2))[0], h_diag[0], h_face[0]]
    out_shape = (
        jax.ShapeDtypeStruct((2, basis, group), BF16),
        jax.ShapeDtypeStruct((4, 2, group), F32),
        jax.ShapeDtypeStruct((1, basis), F32),
    )
    outs = pl.pallas_call(
        functools.partial(kernel, side, bands, chunks, pieces),
        out_shape=out_shape,
        in_specs=[hbm, pl.BlockSpec(memory_space=pltpu.SMEM)] + [hbm] * 3,
        out_specs=(anywhere, vmem, vmem),
        scratch_shapes=[
            pltpu.SMEM((1, faces), jnp.int32),
            pltpu.SMEM((1,), jnp.int32),
            chunked,
            pltpu.VMEM((basis, basis), BF16),
            pltpu.VMEM((faces, basis, basis), BF16),
            pltpu.VMEM((3, 2 * basis, basis), BF16),
            *[chunked] * 6,
            pltpu.VMEM((2, basis, group), BF16),
            pltpu.VMEM((2, basis, group), BF16),
            pltpu.VMEM((half, group), BF16),
            pltpu.VMEM((4, half, basis), BF16),
            pltpu.VMEM((pieces, 2 * block // pieces, group), F32),
            pltpu.VMEM((pieces * peers, 2 * block // pieces, group), BF16),
            pltpu.VMEM((pieces * peers, 2 * block // pieces, group), BF16),
            pltpu.VMEM((side, 16, half), BF16),
            pltpu.VMEM((peers, 16, half), BF16),
            pltpu.VMEM((256, width), F32),
            pltpu.VMEM((bands, 8, 256), F32),
            dma((2 * chunks + 2,)),
            dma((2,)),
            dma((chunks,)),
            dma((4 * chunks,)),
            dma((4 * chunks,)),
            dma((chunks,)),
            dma((chunks,)),
            dma((pieces * peers,)),
            dma((pieces * peers,)),
            dma((peers,)),
            dma((peers,)),
            dma((max(bands - 1, 1),)),
            dma((max(bands - 1, 1),)),
        ],
        compiler_params=pltpu.CompilerParams(
            collective_id=0, has_side_effects=True, vmem_limit_bytes=40 * 2**20
        ),
        name="step",
    )(pltpu.with_memory_space_constraint(adjacency, pltpu.HBM), nbasis, *[pltpu.with_memory_space_constraint(a, pltpu.HBM) for a in arguments[2:]])
    out_psi, out_int, out_den = pl.pallas_call(
        finish,
        out_shape=out_shape,
        in_specs=[anywhere] * 3,
        out_specs=(anywhere,) * 3,
        scratch_shapes=[dma((3,))],
        compiler_params=pltpu.CompilerParams(vmem_limit_bytes=40 * 2**20),
        name="finish",
    )(*outs)
    return jnp.transpose(out_psi, (0, 2, 1))[:, None], out_int, out_den


def build(mesh, side, chunks, pieces):
    bands = mesh.shape["band"]
    return jax.shard_map(
        functools.partial(shards, side, bands, chunks, pieces),
        mesh=mesh,
        in_specs=(
            P(None, "elem", "band", None),
            P("elem", None, None),
            P("elem", None, None, None),
            P("elem", None),
            P("elem"),
        ),
        out_specs=(P(None, "elem", "band", None), P("elem", None, "band"), P("elem", None)),
        check_vma=False,
    )


def solution(mesh):
    return build(mesh, 8, 4, 2)
```

```python
import functools

import jax
import jax.numpy as jnp
from jax import lax
from jax.experimental import pallas as pl
from jax.experimental.pallas import tpu as pltpu
from jax.sharding import PartitionSpec as P

MESH = pl.DeviceIdType.MESH
F32 = jnp.float32
BF16 = jnp.bfloat16
HALF_STEP = 0.1


def dot(a, b):
    return jnp.dot(a, b, preferred_element_type=F32)


def dot_nt(a, b):
    return lax.dot_general(a, b, (((1,), (1,)), ((), ())), preferred_element_type=F32)


def kernel(
    side, bands, chunks, pieces, adj_h, nb_h, psi, hd, hf, out_psi, out_int, out_den,
    adj, nb, psi_v, hd_v, hf_v, hm, t0, t0f, t0n, t1, t1f, t1n, xo, xp, pick, sel, own, gs, gr, s2, s2r, dac, dens,
    load_sem, few_sem, out_sem, h_send, h_recv, p_send, p_recv, g_send, g_recv, r_send, r_recv, d_send, d_recv,
):
    elems = side * side * 2
    faces = hf.shape[0]
    basis = hd.shape[0]
    group = out_psi.shape[2]
    width = group // chunks
    peers = side - 1
    turn = [side // 2 + (k // 2 if k % 2 == 0 else -(k + 1) // 2) for k in range(side)]

    e = lax.axis_index("elem")
    band = lax.axis_index("band")
    core = e % 2
    chip = e // 2
    y, z = chip // side, chip % side
    far = (e + elems - 1 + 2 * core) % elems
    near = e + 1 - 2 * core

    def along(first, r):
        by_y = core if not first else 1 - core
        yy = (y + by_y * r) % side
        zz = (z + (1 - by_y) * r) % side
        return (yy * side + zz) * 2 + core

    firsts = [along(True, r) for r in turn[:-1]]
    seconds = [along(False, r) for r in range(1, side)]
    reach = [r for r in (1, 2, -1, -2) if abs(r) < bands]
    if bands <= 3:
        reach = [1, -1][: bands - 1]

    barrier = pltpu.get_barrier_semaphore()
    everyone = [(far, band), (near, band)]
    everyone += [(d, band) for d in firsts + seconds]
    everyone += [(e, (band + r) % bands) for r in reach]
    for d in everyone:
        pl.semaphore_signal(barrier, inc=1, device_id=d, device_id_type=MESH)

    load_adj = pltpu.make_async_copy(adj_h, adj, few_sem.at[1])
    load_adj.start()
    loads = []
    for i in range(chunks):
        for c in range(2):
            copy = pltpu.make_async_copy(
                psi.at[c, :, pl.ds(i * width, width)], psi_v.at[i, :, pl.ds(c * width, width)], load_sem.at[2 * i + c]
            )
            copy.start()
            loads.append(copy)
    load_hd = pltpu.make_async_copy(hd, hd_v, load_sem.at[2 * chunks])
    load_hf = pltpu.make_async_copy(hf, hf_v, load_sem.at[2 * chunks + 1])
    load_hd.start()
    load_hf.start()

    keep = lax.broadcasted_iota(jnp.int32, (basis, 2 * width), 0) < nb_h[0]

    def halo(sweep, i, src, dst, to_far):
        s = (sweep * 2 + to_far) * chunks + i
        return pltpu.make_async_remote_copy(
            src_ref=src.at[i], dst_ref=dst.at[i], send_sem=h_send.at[s], recv_sem=h_recv.at[s],
            device_id=(far if to_far else near, band), device_id_type=MESH,
        )

    sent = []
    for i in range(chunks):
        loads[2 * i].wait()
        loads[2 * i + 1].wait()
        t0[i] = jnp.where(keep, psi_v[i].astype(F32), 0.0).astype(BF16)
        if i == 0:
            pl.semaphore_wait(barrier, len(everyone))
        for copy in (halo(0, i, t0, t0f, 1), halo(0, i, t0, t0n, 0)):
            copy.start()
            sent.append(copy)

    load_hd.wait()
    load_hf.wait()
    load_adj.wait()
    weights = [[jnp.where(adj[0, f] == s, 1.0, 0.0).astype(F32) for f in range(faces)] for s in (e, far, near)]
    strip = 16

    def prepare(n, carry):
        rows = pl.ds(pl.multiple_of(n * strip, strip), strip)
        low = pl.ds(pl.multiple_of(basis + n * strip, strip), strip)
        valid = lax.broadcasted_iota(jnp.int32, (strip, basis), 0) + n * strip < nb_h[0]
        faces_f32 = [hf_v[f, rows, :].astype(F32) for f in range(faces)]
        for s in range(3):
            total = hd_v[rows, :].astype(F32) if s == 0 else jnp.zeros((strip, basis), F32)
            for f in range(faces):
                total = total + weights[s][f] * faces_f32[f]
            total = jnp.where(valid, total, 0.0)
            high = total.astype(BF16)
            hm[s, rows, :] = high
            hm[s, low, :] = (total - high.astype(F32)).astype(BF16)
        return carry

    lax.fori_loop(0, basis // strip, prepare, 0)

    def image(sweep, i, mine, other, beside):
        halo(sweep, i, mine, beside, 0).wait_recv()
        both = dot(hm[0], mine[i]) + dot(hm[2], beside[i])
        halo(sweep, i, mine, other, 1).wait_recv()
        both = both + dot(hm[1], other[i])
        return both[:basis] + both[basis:]

    for i in range(chunks):
        im = image(0, i, t0, t0f, t0n)
        base = t0[i].astype(F32)
        turned = jnp.concatenate([im[:, width:], -im[:, :width]], axis=1)
        state = (base + (2 * HALF_STEP) * turned).astype(BF16)
        t1[i] = (base + state.astype(F32)).astype(BF16)
        for copy in (halo(1, i, t1, t1f, 1), halo(1, i, t1, t1n, 0)):
            copy.start()
            sent.append(copy)

    block = group // 2 // side
    part = block // pieces
    slab = min(group, 128)
    t = lax.broadcasted_iota(jnp.int32, (group // 2, slab), 0)
    o = lax.broadcasted_iota(jnp.int32, (group // 2, slab), 1)

    def split(v, size):
        return v >> (size.bit_length() - 1), v & (size - 1)

    k, j = split(t, part)
    h, k = split(k, side)
    up, odd = split(k, 2)
    r = side // 2 + jnp.where(odd == 0, up, -1 - up)
    d = ((1 - core) * y + core * z + r) & (side - 1)
    q, four = split(h * part + j, 4)
    orbital = ((1 - core) * (d * side + q) + core * (q * side + d)) * 8 + core * 4 + four
    for n in range(group // slab):
        pick[:, n * slab : (n + 1) * slab] = jnp.where(orbital == o + n * slab, 1.0, 0.0).astype(BF16)

    def joined(source, c):
        return jnp.concatenate([source[i, c] for i in range(chunks)], axis=1)

    def to_partner(i):
        return pltpu.make_async_remote_copy(
            src_ref=xo.at[i], dst_ref=xp.at[i], send_sem=p_send.at[i], recv_sem=p_recv.at[i],
            device_id=(near, band), device_id_type=MESH,
        )

    stores = []
    dac[...] = jnp.zeros_like(dac)
    for i in range(chunks):
        im = image(1, i, t1, t1f, t1n)
        base = t0[i].astype(F32)
        lanes = pl.ds(i * width, width)
        real = (base[:, :width] + HALF_STEP * im[:, width:]).astype(BF16)
        imag = (base[:, width:] - HALF_STEP * im[:, :width]).astype(BF16)
        xo[i, 0] = real
        xo[i, 1] = imag
        copy = to_partner(i)
        copy.start()
        sent.append(copy)
        copy = pltpu.make_async_copy(xo.at[i], out_psi.at[:, :, lanes], out_sem.at[i])
        copy.start()
        stores.append(copy)
        real, imag = real.astype(F32), imag.astype(F32)
        dac[:basis, :] += real * real + imag * imag

    for c in range(2):
        sel[c] = dot_nt(pick[...], joined(xo, c)).astype(BF16)
    column = jnp.transpose(dac[...])
    some = column[0:8]
    for n in range(1, width // 8):
        some = some + column[8 * n : 8 * n + 8]
    dens[band] = some

    def density(n, to, slot):
        slot = (band + slot) % bands
        return pltpu.make_async_remote_copy(
            src_ref=dens.at[slot], dst_ref=dens.at[slot], send_sem=d_send.at[n], recv_sem=d_recv.at[n],
            device_id=(e, (band + to) % bands), device_id_type=MESH,
        )

    for n, r in enumerate(reach):
        copy = density(n, r, 0)
        copy.start()
        sent.append(copy)
    passed = [(2, -2), (2, -1), (-2, 1)] if bands == 8 else []

    for i in range(chunks):
        to_partner(i).wait_recv()
    for c in range(2):
        sel[2 + c] = dot_nt(pick[...], joined(xp, c)).astype(BF16)

    def first(h, k):
        s = h * peers + k
        return pltpu.make_async_remote_copy(
            src_ref=gs.at[s], dst_ref=gr.at[s], send_sem=g_send.at[s], recv_sem=g_recv.at[s],
            device_id=(firsts[k], band), device_id_type=MESH,
        )

    high = side * part
    for h in range(pieces):
        rows = pl.ds(h * high, high)
        total = None
        for source, at in ((xo, 0), (xp, 2)):
            left, right = sel[at, rows, :], sel[at + 1, rows, :]
            term = dot(jnp.concatenate([left, right], axis=0), joined(source, 0))
            term = term + dot(jnp.concatenate([right, -left], axis=0), joined(source, 1))
            total = term if total is None else total + term
        for k in range(side):
            both = jnp.concatenate(
                [total[k * part : (k + 1) * part], total[high + k * part : high + (k + 1) * part]], axis=0
            )
            if k < peers:
                gs[h * peers + k] = both.astype(BF16)
                copy = first(h, k)
                copy.start()
                sent.append(copy)
            else:
                own[h] = both

    place = core * y + (1 - core) * z
    upper = lax.broadcasted_iota(jnp.int32, (8, group), 0) < 4

    def second(q, r):
        return pltpu.make_async_remote_copy(
            src_ref=s2.at[q], dst_ref=s2r.at[r - 1], send_sem=r_send.at[r - 1], recv_sem=r_recv.at[r - 1],
            device_id=(along(False, r), band), device_id_type=MESH,
        )

    for h in range(pieces):
        for k in range(peers):
            first(h, k).wait_recv()
        for m in range(part // 8):
            tiles = []
            for at in (8 * m, part + 8 * m):
                tile = own[h, at : at + 8, :]
                for k in range(peers):
                    tile = tile + gr[h * peers + k, at : at + 8, :].astype(F32)
                tiles.append(tile)
            q = h * (part // 4) + 2 * m
            for to, tile in (
                (q, jnp.where(upper, tiles[0], pltpu.roll(tiles[1], 4, 0))),
                (q + 1, jnp.where(upper, pltpu.roll(tiles[0], 4, 0), tiles[1])),
            ):
                s2[to] = jnp.concatenate([tile[:, : group // 2], tile[:, group // 2 :]], axis=0).astype(BF16)
            for to in (q, q + 1):
                r = (to + side - place) % side

                @pl.when(r != 0)
                def _(to=to, r=r):
                    second(to, r).start()

        if h == 0:
            for n, r in enumerate(reach):
                density(n, r, -r).wait_recv()
            for n, (to, slot) in enumerate(passed):
                copy = density(len(reach) + n, to, slot)
                copy.start()
                sent.append(copy)

    result = s2[place].astype(F32)
    for r in range(1, side):
        second((place + r) % side, r).wait_recv()
        result = result + s2r[r - 1].astype(F32)
    result = jnp.concatenate([result[:8], result[8:]], axis=1) * (1.0 / (elems * basis))
    for n in range(4):
        out_int[n, 0:1, :] = result[n : n + 1]
        out_int[n, 1:2, :] = result[4 + n : 5 + n]
    for n, (to, slot) in enumerate(passed):
        density(len(reach) + n, to, slot - to).wait_recv()
    some = dens[0]
    for n in range(1, bands):
        some = some + dens[n]
    whole = jnp.sum(some, axis=0, keepdims=True) * (1.0 / (group * bands))
    out_den[...] = whole[:, :basis]

    for r in range(1, side):
        second((place + r) % side, r).wait_send()
    for copy in stores:
        copy.wait()
    for copy in sent:
        copy.wait_send()


def finish(*refs):
    copies = [pltpu.make_async_copy(refs[n], refs[3 + n], refs[6].at[n]) for n in (1, 2)]
    rows = refs[0].shape[1] // 3
    for n in range(6):
        part = (n // 3, pl.ds(n % 3 * rows, rows))
        copies.append(pltpu.make_async_copy(refs[0].at[part], refs[3].at[part], refs[6].at[3 + n]))
    for copy in copies:
        copy.start()
    for copy in copies:
        copy.wait()


def shards(side, bands, chunks, pieces, psi, h_diag, h_face, adjacency, nbasis):
    group, basis = psi.shape[2], psi.shape[3]
    faces = h_face.shape[1]
    width = group // chunks
    half = group // 2
    block = half // side
    peers = side - 1
    dma = pltpu.SemaphoreType.DMA
    anywhere = pl.BlockSpec(memory_space=pl.ANY)
    hbm = pl.BlockSpec(memory_space=pltpu.HBM)
    vmem = pl.BlockSpec(memory_space=pltpu.VMEM)
    chunked = pltpu.VMEM((chunks, basis, 2 * width), BF16)
    arguments = [adjacency, nbasis, jnp.transpose(psi, (1, 0, 3, 2))[0], h_diag[0], h_face[0]]
    out_shape = (
        jax.ShapeDtypeStruct((2, basis, group), BF16),
        jax.ShapeDtypeStruct((4, 2, group), F32),
        jax.ShapeDtypeStruct((1, basis), F32),
    )
    outs = pl.pallas_call(
        functools.partial(kernel, side, bands, chunks, pieces),
        out_shape=out_shape,
        in_specs=[hbm, pl.BlockSpec(memory_space=pltpu.SMEM)] + [hbm] * 3,
        out_specs=(anywhere, vmem, vmem),
        scratch_shapes=[
            pltpu.SMEM((1, faces), jnp.int32),
            pltpu.SMEM((1,), jnp.int32),
            chunked,
            pltpu.VMEM((basis, basis), BF16),
            pltpu.VMEM((faces, basis, basis), BF16),
            pltpu.VMEM((3, 2 * basis, basis), BF16),
            *[chunked] * 6,
            pltpu.VMEM((chunks, 2, basis, width), BF16),
            pltpu.VMEM((chunks, 2, basis, width), BF16),
            pltpu.VMEM((half, group), BF16),
            pltpu.VMEM((4, half, basis), BF16),
            pltpu.VMEM((pieces, 2 * block // pieces, group), F32),
            pltpu.VMEM((pieces * peers, 2 * block // pieces, group), BF16),
            pltpu.VMEM((pieces * peers, 2 * block // pieces, group), BF16),
            pltpu.VMEM((side, 16, half), BF16),
            pltpu.VMEM((peers, 16, half), BF16),
            pltpu.VMEM((256, width), F32),
            pltpu.VMEM((bands, 8, 256), F32),
            dma((2 * chunks + 2,)),
            dma((2,)),
            dma((chunks,)),
            dma((4 * chunks,)),
            dma((4 * chunks,)),
            dma((chunks,)),
            dma((chunks,)),
            dma((pieces * peers,)),
            dma((pieces * peers,)),
            dma((peers,)),
            dma((peers,)),
            dma((max(bands - 1, 1),)),
            dma((max(bands - 1, 1),)),
        ],
        compiler_params=pltpu.CompilerParams(
            collective_id=0, has_side_effects=True, vmem_limit_bytes=40 * 2**20
        ),
        name="step",
    )(pltpu.with_memory_space_constraint(adjacency, pltpu.HBM), nbasis, *[pltpu.with_memory_space_constraint(a, pltpu.HBM) for a in arguments[2:]])
    out_psi, out_int, out_den = pl.pallas_call(
        finish,
        out_shape=out_shape,
        in_specs=[anywhere] * 3,
        out_specs=(anywhere,) * 3,
        scratch_shapes=[dma((9,))],
        compiler_params=pltpu.CompilerParams(vmem_limit_bytes=40 * 2**20),
        name="finish",
    )(*outs)
    return jnp.transpose(out_psi, (0, 2, 1))[:, None], out_int, out_den


def build(mesh, side, chunks, pieces):
    bands = mesh.shape["band"]
    return jax.shard_map(
        functools.partial(shards, side, bands, chunks, pieces),
        mesh=mesh,
        in_specs=(
            P(None, "elem", "band", None),
            P("elem", None, None),
            P("elem", None, None, None),
            P("elem", None),
            P("elem"),
        ),
        out_specs=(P(None, "elem", "band", None), P("elem", None, "band"), P("elem", None)),
        check_vma=False,
    )


def solution(mesh):
    return build(mesh, 8, 4, 2)
```
